768 devices in a mesh: row: 16 (over x_hi, y), rep: 48 (over z, x_lo, core).
Axes of the slice: x: 4 (x_hi: 2, x_lo: 2; x = x_hi * 2 + x_lo), y: 8, z: 12, core: 2. Of those that a mesh axis runs over, the one named last changes fastest.
Arguments:
- node_features: bfloat16 [196608, 128], P(('row', 'rep')), may hold values from -6 to 6
- layer_weight: bfloat16 [128, 256], replicated, may hold values from -0.5 to 0.5
- tile_values: bfloat16 [16, 768, 8, 128, 128], P('row', 'rep'), may hold values from -0.078125 to 0.078125
- tile_positions: int32 [16, 768, 8], P('row', 'rep'), may hold values from 0 to 191, as said below
- section_tile_count: int32 [16, 768], P('row', 'rep'), may hold values from 1 to 8, as said below
- out_cotangent: bfloat16 [196608, 256], P(('row', 'rep')), may hold values from -0.019897461 to 0.019897461
Outputs:
- mixed_out: bfloat16 [196608, 256], P(('row', 'rep'))
- summed_grad: float32 [128, 256], replicated
The draws below stay inside these ranges and needn't reach their ends.
Inputs may be any that keep to these rules, and one draw needn't show every extreme that they name: `tile_positions`: within one slab, replica and section the live codes are distinct; a code p names tile row p // 2 of the slab's 48 * 2 tile rows and tile column p % 2 of the section's node block. `section_tile_count`: every device (one slab and replica) has one section with all 8 slots live.
All inputs are finite; a program needn't handle non-finite values.
Results may differ from the reference program's by a relative error of at most 0.0049.
Values may be sent and summed in bfloat16 or wider, within the bound.
A program may use at most 32 MiB of HBM per device.

```python
import jax
import jax.numpy as jnp
from jax import lax

FEATURES = 128
HIDDEN_UNITS = 256
TILE = 128
DEVICE_BLOCKS = 2
CAPACITY = 8
NODES = 196608
N_ROW = 16
N_REP = 48


def draw_tile_positions(key, part):
    key = jax.random.fold_in(key, 11)
    total = N_ROW * N_REP * N_ROW
    keys = jax.random.split(key, total)
    perms = jax.vmap(lambda single: jax.random.permutation(single, N_REP * DEVICE_BLOCKS * DEVICE_BLOCKS))(keys)
    return perms[:, :CAPACITY].reshape(N_ROW, N_REP * N_ROW, CAPACITY).astype(jnp.int32)


def draw_section_tile_count(key, part):
    key = jax.random.fold_in(key, 7)
    first_key, second_key, third_key = jax.random.split(key, 3)
    load = jax.random.randint(first_key, (N_ROW, N_REP, 1), 1, 5)
    raw = jax.random.randint(second_key, (N_ROW, N_REP, N_ROW), 0, 1 << 20)
    level = load + raw % (3 * load + 1)
    counts = jnp.maximum(1, level * CAPACITY // 16)
    counts = jnp.minimum(counts, CAPACITY)
    full_section = jax.random.randint(third_key, (N_ROW, N_REP, 1), 0, N_ROW)
    section_ids = jnp.arange(N_ROW, dtype=jnp.int32)[None, None, :]
    counts = jnp.where(section_ids == full_section, CAPACITY, counts)
    return counts.reshape(N_ROW, N_REP * N_ROW).astype(jnp.int32)


def level_of(rng, dims, cuts, least, high):
    level = 1.0
    for position, shards_of in cuts:
        steps = jax.random.uniform(jax.random.fold_in(jax.random.fold_in(rng, 6), position), (shards_of,), jnp.float32, least / len(cuts), high / len(cuts))
        level = level * jnp.repeat(jnp.exp(steps), dims[position] // shards_of).reshape((-1,) + (1,) * (len(dims) - 1 - position))
    return level


def bell_draw(stream_key, extent, width, reach, cuts=(), kind=jnp.bfloat16):
    array = width * jax.random.normal(stream_key, extent, jnp.float32)
    if cuts:
        array = array * level_of(stream_key, extent, cuts, -0.22, 0.18)
    return jnp.clip(array, -reach, reach).astype(kind)


def setup_inputs(seed: int = 0) -> dict:
    arg_keys = jax.random.split(jax.random.key(seed), 7)
    return {
        "node_features": bell_draw(arg_keys[0], (NODES, FEATURES), 1.0, 6.0, ((0, 768),)),
        "layer_weight": bell_draw(arg_keys[1], (FEATURES, HIDDEN_UNITS), FEATURES ** -0.5, 0.5),
        "tile_values": bell_draw(arg_keys[2], (N_ROW, N_REP * N_ROW, CAPACITY, TILE, TILE), (TILE * N_ROW * 3) ** -0.5, 0.078125, ((0, 16), (1, 48))),
        "tile_positions": draw_tile_positions(jax.random.fold_in(arg_keys[6], 71), 0),
        "section_tile_count": draw_section_tile_count(jax.random.fold_in(arg_keys[6], 71), 0),
        "out_cotangent": bell_draw(arg_keys[5], (NODES, HIDDEN_UNITS), 0.003, 0.019897461, ((0, 768),)),
    }


def reference(node_features, layer_weight, tile_values, tile_positions, section_tile_count, out_cotangent):
    blocks_all = node_features.reshape(N_ROW, N_REP, DEVICE_BLOCKS, TILE, FEATURES)
    values_all = tile_values.reshape(N_ROW, N_REP, N_ROW, CAPACITY, TILE, TILE)
    placed_all = tile_positions.reshape(N_ROW, N_REP, N_ROW, CAPACITY)
    counts_all = section_tile_count.reshape(N_ROW, N_REP, N_ROW)
    section_ids = jnp.arange(N_ROW, dtype=jnp.int32)
    slot_ids = jnp.arange(CAPACITY, dtype=jnp.int32)

    def slab_sum(slab_index):
        def replica(rep_index, running):
            adjacency_values = values_all[slab_index, rep_index].astype(jnp.float32)
            placed = placed_all[slab_index, rep_index]
            living = slot_ids[None, :] < counts_all[slab_index, rep_index][:, None]
            section_rows = blocks_all[:, rep_index].astype(jnp.float32)
            selected_tiles = section_rows[section_ids[:, None], placed % DEVICE_BLOCKS]
            tile_products = jnp.einsum("scab,scbf->scaf", adjacency_values, selected_tiles)
            tile_products = jnp.where(living[:, :, None, None], tile_products, jnp.zeros_like(tile_products))
            target = (placed // DEVICE_BLOCKS).reshape(-1).astype(jnp.int32)
            return running.at[target].add(tile_products.reshape(-1, TILE, FEATURES))

        start_sum = jnp.zeros((N_REP * DEVICE_BLOCKS, TILE, FEATURES), jnp.float32)
        return lax.fori_loop(0, N_REP, replica, start_sum)

    aggregate = lax.map(slab_sum, section_ids).reshape(N_ROW * N_REP * DEVICE_BLOCKS * TILE, FEATURES)
    mixed_out = jnp.dot(aggregate.astype(jnp.bfloat16), layer_weight, preferred_element_type=jnp.float32).astype(jnp.bfloat16)
    summed_grad = jnp.einsum("nf,nh->fh", aggregate, out_cotangent.astype(jnp.float32), precision=lax.Precision.HIGHEST)
    return mixed_out, summed_grad
```

```python
import functools

import jax
import jax.numpy as jnp
from jax import lax
from jax.experimental import pallas as pl
from jax.experimental.pallas import tpu as pltpu
from jax.sharding import PartitionSpec as P

MESH = pl.DeviceIdType.MESH
F32, BF16 = jnp.float32, jnp.bfloat16
XH, XL, CORES = 2, 2, 2


def place(ny):
    row, rep = lax.axis_index("row"), lax.axis_index("rep")
    return row // ny, lax.rem(row, ny), rep // 4, lax.rem(rep // 2, 2), lax.rem(rep, 2)


def greet(peers):
    barrier = pltpu.get_barrier_semaphore()
    for peer in peers:
        pl.semaphore_signal(barrier, inc=1, device_id=peer, device_id_type=MESH)
    pl.semaphore_wait(barrier, len(peers))


def gather_kernel(ny, x_ref, out_ref, send_sem, recv_sem, own_sem):
    xh, y, z, xl, c = place(ny)
    row, rep = lax.axis_index("row"), lax.axis_index("rep")
    half = ny // 2
    partner = ((1 - xh) * ny + y, rep)
    up = (xh * ny + lax.rem(y + 1, ny), rep)
    down = (xh * ny + lax.rem(y + ny - 1, ny), rep)
    greet([partner] + ([up, down] if ny > 2 else [up]))
    own = pltpu.make_async_copy(x_ref, out_ref.at[row], own_sem)
    own.start()
    started = []

    def send(src, slot, peer, k):
        copy = pltpu.make_async_remote_copy(
            src, out_ref.at[slot], send_sem.at[k], recv_sem.at[k], device_id=peer, device_id_type=MESH
        )
        copy.start()
        started.append(copy)
        return copy

    def slot_of(side, shift):
        return side * ny + lax.rem(y + shift + ny, ny)

    count = 1
    flows = [(0, 1, half), (0, -1, half - 1), (1, 1, half - 1), (1, -1, half)]
    last = [None] * 4
    cross = None
    for step in range(half):
        for f, (side, way, steps) in enumerate(flows):
            if step >= steps:
                continue
            which = xh if side == 0 else 1 - xh
            slot = slot_of(which, -way * step)
            src = out_ref.at[slot]
            if step == 0:
                if side == 0:
                    src = x_ref
                elif cross is not None and last[2] is None and last[3] is None:
                    cross.wait_recv()
            else:
                last[f].wait_recv()
            last[f] = send(src, slot, up if way == 1 else down, count)
            count += 1
            if step == 0 and f == 0:
                cross = send(x_ref, row, partner, 0)
    if ny == 2:
        pass
    own.wait()
    for f in range(4):
        if last[f] is not None:
            last[f].wait_recv()
    for copy in started:
        copy.wait_send()


def gather(x, ny):
    copies = 1 + 2 * (ny - 1)
    return pl.pallas_call(
        functools.partial(gather_kernel, ny),
        out_shape=jax.ShapeDtypeStruct((XH * ny,) + x.shape, x.dtype),
        in_specs=[pl.BlockSpec(memory_space=pltpu.VMEM)],
        out_specs=pl.BlockSpec(memory_space=pltpu.VMEM),
        scratch_shapes=[
            pltpu.SemaphoreType.DMA((copies,)),
            pltpu.SemaphoreType.DMA((copies,)),
            pltpu.SemaphoreType.DMA,
        ],
        compiler_params=pltpu.CompilerParams(
            collective_id=0, has_side_effects=True, vmem_limit_bytes=16 << 20
        ),
        name="gather_features",
    )(x)


def section_kernel(tiles_all, pos_ref, cnt_ref, tile_ref, x_ref, own_ref, oth_ref, acc, prod):
    j = pl.program_id(0)
    sections = pl.num_programs(0)
    cap, edge = tile_ref.shape[1], tile_ref.shape[2]
    core = lax.rem(lax.axis_index("rep"), 2)
    half = tiles_all // 2

    @pl.when(j == 0)
    def _():
        def clear(t, carry):
            acc[t] = jnp.zeros(acc.shape[1:], F32)
            return carry

        lax.fori_loop(0, tiles_all, clear, 0)

    both = jnp.concatenate([x_ref[j, :edge], x_ref[j, edge:]], axis=1)
    tiles = tile_ref[0].reshape(cap * edge, edge)
    prod[...] = jnp.dot(tiles, both, preferred_element_type=F32)
    live = cnt_ref[j]
    for s in range(cap):
        p = pos_ref[j, s]
        t = p // 2
        chunk = t // 2
        spot = jnp.where(lax.rem(chunk, 2) == core, 0, half) + (chunk // 2) * 2 + lax.rem(t, 2)
        spot = jnp.where(s < live, spot, tiles_all)
        lane = pl.multiple_of(lax.rem(p, 2) * edge, edge)
        acc[spot] += prod[s * edge : (s + 1) * edge, pl.ds(lane, edge)]

    @pl.when(j == sections - 1)
    def _():
        def out(k, carry):
            own_ref[k] = acc[k]
            oth_ref[k] = acc[half + k].astype(BF16)
            return carry

        lax.fori_loop(0, half, out, 0)


def section_sums(tiles, positions, counts, rows, reps):
    sections, cap, edge, _ = tiles.shape
    tiles_all = reps * 2
    return pl.pallas_call(
        functools.partial(section_kernel, tiles_all),
        out_shape=(
            jax.ShapeDtypeStruct((tiles_all // 2, edge, edge), F32),
            jax.ShapeDtypeStruct((tiles_all // 2, edge, edge), BF16),
        ),
        grid_spec=pltpu.PrefetchScalarGridSpec(
            num_scalar_prefetch=2,
            grid=(sections,),
            in_specs=[
                pl.BlockSpec((1, cap, edge, edge), lambda j, *_: (j, 0, 0, 0)),
                pl.BlockSpec(rows.shape, lambda j, *_: (0, 0, 0)),
            ],
            out_specs=(
                pl.BlockSpec((tiles_all // 2, edge, edge), lambda j, *_: (0, 0, 0)),
                pl.BlockSpec((tiles_all // 2, edge, edge), lambda j, *_: (0, 0, 0)),
            ),
            scratch_shapes=[
                pltpu.VMEM((tiles_all + 1, edge, edge), F32),
                pltpu.VMEM((cap * edge, 2 * edge), F32),
            ],
        ),
        compiler_params=pltpu.CompilerParams(vmem_limit_bytes=40 << 20),
        name="section_products",
    )(positions, counts, tiles, rows)


def reduce_kernel(
    ny, nz, own_ref, oth_ref, w_ref, g_ref, mixed_ref, grad_ref,
    cbuf, sbuf, rbuf, xsend, xrecv, gbuf, r1, hbuf, r2, vbuf, r3, ubuf, r4, tbuf, r5, r6,
    c_s, c_r, z_s, z_r, x_s, x_r, a_s, a_r,
):
    xh, y, z, xl, c = place(ny)
    row, rep = lax.axis_index("row"), lax.axis_index("rep")
    half = nz // 2
    core_peer = (row, rep + 1 - 2 * c)
    x_peer = (row, z * 4 + (1 - xl) * 2 + c)

    def z_peer(d):
        return (row, lax.rem(z + d + nz, nz) * 4 + xl * 2 + c)

    def y_peer(d):
        return (xh * ny + lax.rem(y + d, ny), rep)

    x = xh * 2 + xl

    def x4_peer(d):
        q = lax.rem(x + d, 4)
        return ((q // 2) * ny + y, z * 4 + lax.rem(q, 2) * 2 + c)

    greet(
        [core_peer]
        + [z_peer(d) for d in range(1, nz)]
        + [y_peer(d) for d in range(1, ny)]
        + [x4_peer(d) for d in range(1, 4)]
    )
    started = []

    def send(src, dst, s_sem, r_sem, peer):
        copy = pltpu.make_async_remote_copy(src, dst, s_sem, r_sem, device_id=peer, device_id_type=MESH)
        copy.start()
        started.append(copy)
        return copy

    order = [half]
    for d in range(half - 1, 0, -1):
        order += [d, -d]
    order.append(0)
    cross = {}
    for k, d in enumerate(order):
        at = lax.rem(z + d + nz, nz)
        cross[d] = send(oth_ref.at[at], cbuf.at[at], c_s.at[k], c_r.at[k], core_peer)
    ready = set()

    def mine(d, side):
        if d == -half:
            d = half
        if d not in ready:
            cross[d].wait_recv()
            ready.add(d)
        at = lax.rem(z + d + nz, nz)
        return own_ref[at, side] + cbuf[at, side].astype(F32)

    side_a, side_b = 1 - xl, xl
    flows = [(0, 1, half), (0, -1, half - 1), (1, 1, half - 1), (1, -1, half)]
    last = [None] * 4
    count = 0
    for step in range(half):
        for f, (side, way, steps) in enumerate(flows):
            if step < half - steps:
                continue
            distance = half - step
            total = mine(way * distance, side_a if side == 0 else side_b)
            if last[f] is not None:
                last[f][0].wait_recv()
                total = total + rbuf[last[f][1]].astype(F32)
            sbuf[count] = total.astype(BF16)
            last[f] = (send(sbuf.at[count], rbuf.at[count], z_s.at[count], z_r.at[count], z_peer(way)), count)
            count += 1

    def finish(side, first, second):
        total = mine(0, side)
        for f in (first, second):
            if last[f] is not None:
                last[f][0].wait_recv()
                total = total + rbuf[last[f][1]].astype(F32)
        return total

    xsend[...] = finish(side_a, 0, 1)
    over = send(xsend, xrecv, x_s, x_r, x_peer)
    kept = finish(side_b, 2, 3)
    over.wait_recv()
    aggregate = kept + xrecv[...]
    gbuf[...] = lax.dot_general(
        aggregate, g_ref[...].astype(F32), (((0,), (0,)), ((), ())),
        precision=lax.Precision.HIGHEST, preferred_element_type=F32,
    )

    used = [0]

    def pair():
        k = used[0]
        used[0] += 1
        return a_s.at[k], a_r.at[k]

    hrows = gbuf.shape[0] // 2
    piece = hrows // ny
    first = send(gbuf.at[pl.ds(pl.multiple_of((1 - c) * hrows, hrows), hrows)], r1, *pair(), core_peer)
    mixed_ref[...] = jnp.dot(
        aggregate.astype(BF16), w_ref[...], preferred_element_type=F32
    ).astype(BF16)
    first.wait_recv()
    hbuf[...] = (gbuf[pl.ds(pl.multiple_of(c * hrows, hrows), hrows)] + r1[...]).reshape(hbuf.shape)

    def spread(src_of, slots, mine_at, peers):
        copies = []
        for k, peer in enumerate(peers):
            copies.append(send(src_of(k + 1), slots.at[mine_at], *pair(), peer))
        return copies

    def total_of(slots, n):
        total = slots[0]
        for k in range(1, n):
            total = total + slots[k]
        return total

    r2[y] = hbuf[y]
    for copy in spread(lambda d: hbuf.at[lax.rem(y + d, ny)], r2, y, [y_peer(d) for d in range(1, ny)]):
        copy.wait_recv()
    vbuf[...] = total_of(r2, ny)
    r3[x] = vbuf[...]
    for copy in spread(lambda d: vbuf, r3, x, [x4_peer(d) for d in range(1, 4)]):
        copy.wait_recv()
    ubuf[...] = total_of(r3, 4)
    r4[z] = ubuf[...]
    for copy in spread(lambda d: ubuf, r4, z, [z_peer(d) for d in range(1, nz)]):
        copy.wait_recv()
    tbuf[...] = total_of(r4, nz)
    r5[y] = tbuf[...]
    back = spread(lambda d: tbuf, r5, y, [y_peer(d) for d in range(1, ny)])
    other = [send(tbuf, r6.at[y], *pair(), core_peer)]
    for d, copy in enumerate(back):
        copy.wait_recv()
        at = lax.rem(y - (d + 1) + ny, ny)
        other.append(send(r5.at[at], r6.at[at], *pair(), core_peer))
    for copy in other:
        copy.wait_recv()
    grad_ref[pl.ds(pl.multiple_of(c * hrows, hrows), hrows)] = r5[...].reshape(hrows, -1)
    grad_ref[pl.ds(pl.multiple_of((1 - c) * hrows, hrows), hrows)] = r6[...].reshape(hrows, -1)
    for copy in started:
        copy.wait_send()


def reduce_all(own, oth, w, g, ny, nz):
    f, h = w.shape
    rows = g.shape[0]
    copies = nz - 1 + nz - 1
    hrows = f // 2
    piece = hrows // ny
    small = 1 + 2 * (ny - 1) + 3 + (nz - 1) + ny
    dma = pltpu.SemaphoreType.DMA
    return pl.pallas_call(
        functools.partial(reduce_kernel, ny, nz),
        out_shape=(
            jax.ShapeDtypeStruct((rows, h), BF16),
            jax.ShapeDtypeStruct((f, h), F32),
        ),
        in_specs=[pl.BlockSpec(memory_space=pltpu.VMEM)] * 4,
        out_specs=(pl.BlockSpec(memory_space=pltpu.VMEM),) * 2,
        scratch_shapes=[
            pltpu.VMEM((nz, 2, rows, f), BF16),
            pltpu.VMEM((copies, rows, f), BF16),
            pltpu.VMEM((copies, rows, f), BF16),
            pltpu.VMEM((rows, f), F32),
            pltpu.VMEM((rows, f), F32),
            pltpu.VMEM((f, h), F32),
            pltpu.VMEM((hrows, h), F32),
            pltpu.VMEM((ny, piece, h), F32),
            pltpu.VMEM((ny, piece, h), F32),
            pltpu.VMEM((piece, h), F32),
            pltpu.VMEM((4, piece, h), F32),
            pltpu.VMEM((piece, h), F32),
            pltpu.VMEM((nz, piece, h), F32),
            pltpu.VMEM((piece, h), F32),
            pltpu.VMEM((ny, piece, h), F32),
            pltpu.VMEM((ny, piece, h), F32),
            dma((nz,)), dma((nz,)), dma((copies,)), dma((copies,)), dma, dma, dma((small,)), dma((small,)),
        ],
        compiler_params=pltpu.CompilerParams(
            collective_id=1, has_side_effects=True, vmem_limit_bytes=40 << 20
        ),
        name="reduce_and_grad",
    )(own.reshape(nz, 2, rows, f), oth.reshape(nz, 2, rows, f), w, g)


def body(node_features, layer_weight, tile_values, tile_positions, section_tile_count, out_cotangent):
    ny = lax.axis_size("row") // XH
    reps = lax.axis_size("rep")
    nz = reps // (XL * CORES)
    rows = gather(node_features, ny)
    own, oth = section_sums(tile_values[0], tile_positions[0], section_tile_count[0], rows, reps)
    return reduce_all(own, oth, layer_weight, out_cotangent, ny, nz)


def solution(mesh):
    placed = (
        P(("row", "rep"), None),
        P(),
        P("row", "rep", None, None, None),
        P("row", "rep", None),
        P("row", "rep"),
        P(("row", "rep"), None),
    )
    return jax.shard_map(
        body, mesh=mesh, in_specs=placed, out_specs=(P(("row", "rep"), None), P()), check_vma=False
    )
```

```python
import functools

import jax
import jax.numpy as jnp
from jax import lax
from jax.experimental import pallas as pl
from jax.experimental.pallas import tpu as pltpu
from jax.sharding import PartitionSpec as P

MESH = pl.DeviceIdType.MESH
F32, BF16, I32 = jnp.float32, jnp.bfloat16, jnp.int32
XH, XL, CORES = 2, 2, 2
PIECES = 2


def iota(shape, dim):
    return lax.broadcasted_iota(I32, shape, dim)


def sort_slots(pos, cnt, tiles_all, width):
    n, cap = pos.shape
    slots = n * cap
    diag = iota((n, n), 0) == iota((n, n), 1)
    count = jnp.sum(jnp.where(diag, jnp.broadcast_to(cnt, (n, n)), 0), axis=1, keepdims=True)
    slot = iota((n, cap), 1)
    key = jnp.where(slot < count, lax.div(pos, 2), tiles_all)
    code = (key * slots + iota((n, cap), 0) * cap + slot) * 2 + lax.rem(pos, 2)
    spread = jnp.broadcast_to(code[:, None, :], (n, cap, cap))
    picked = jnp.where(iota((n, cap, cap), 1) == iota((n, cap, cap), 2), spread, 0)
    column = jnp.sum(picked, axis=2, keepdims=True).reshape(slots, 1)
    grid = jnp.broadcast_to(column, (slots, slots))
    lane = iota((slots, slots), 1)
    line = jnp.sum(jnp.where(iota((slots, slots), 0) == lane, grid, 0), axis=0, keepdims=True)
    rank = jnp.sum(jnp.where(line < grid, 1, 0), axis=1, keepdims=True)
    ordered = jnp.sum(jnp.where(rank == lane, grid, 0), axis=0, keepdims=True)
    rows = lax.div(jnp.broadcast_to(column, (slots, width)), 2 * slots)
    ends = jnp.sum(jnp.where(rows <= iota((slots, width), 1), 1, 0), axis=0, keepdims=True)
    return ordered, ends


def kernel(
    ny, nz, reach, x_ref, w_ref, tile_ref, pos_ref, cnt_ref, g_ref, mixed_ref, grad_ref,
    tiles, xall, prod, runs, codes_v, ends_v, codes, ends, gall, oth, cbuf, sbuf, rbuf, mbuf,
    xsend, xrecv, gbuf, r1, hbuf, r2, vbuf, r3, ubuf, r4, tbuf, r5, r6,
    t_s, i_s, ag_s, ag_r, g_s, g_r, c_s, c_r, z_s, z_r, x_s, x_r, a_s, a_r,
):
    row, rep = lax.axis_index("row"), lax.axis_index("rep")
    xh, y = row // ny, lax.rem(row, ny)
    z, xl, c = rep // 4, lax.rem(rep // 2, 2), lax.rem(rep, 2)
    x = xh * 2 + xl
    half, yhalf = nz // 2, ny // 2
    n, cap, edge = tiles.shape[0], tiles.shape[1], tiles.shape[2]
    slots = n * cap

    partner = ((1 - xh) * ny + y, rep)
    core_peer = (row, rep + 1 - 2 * c)
    x_peer = (row, z * 4 + (1 - xl) * 2 + c)

    def z_peer(d):
        return (row, lax.rem(z + d + nz, nz) * 4 + xl * 2 + c)

    def y_peer(d):
        return (xh * ny + lax.rem(y + d + ny, ny), rep)

    def x4_peer(d):
        q = lax.rem(x + d, 4)
        return ((q // 2) * ny + y, z * 4 + lax.rem(q, 2) * 2 + c)

    started = []

    def send(src, dst, s_sem, r_sem, peer):
        copy = pltpu.make_async_remote_copy(src, dst, s_sem, r_sem, device_id=peer, device_id_type=MESH)
        copy.start()
        started.append(copy)
        return copy

    load_tiles = pltpu.make_async_copy(tile_ref, tiles, t_s)
    load_tiles.start()
    barrier = pltpu.get_barrier_semaphore()
    peers = [partner, core_peer, x_peer, z_peer(1), y_peer(1)]
    if nz > 2:
        peers.append(z_peer(-1))
    if ny > 2:
        peers.append(y_peer(-1))
    for peer in peers:
        pl.semaphore_signal(barrier, inc=1, device_id=peer, device_id_type=MESH)
    tiles_all = nz * 8
    codes_v[...], ends_v[...] = sort_slots(pos_ref[0], cnt_ref[...], tiles_all, ends_v.shape[1])
    to_scalar = [pltpu.make_async_copy(codes_v, codes, i_s.at[0]), pltpu.make_async_copy(ends_v, ends, i_s.at[1])]
    for copy in to_scalar:
        copy.start()
    load_tiles.wait()
    pl.semaphore_wait(barrier, len(peers))

    flows = [(0, 1, yhalf), (0, -1, yhalf - 1), (1, 1, yhalf - 1), (1, -1, yhalf)]
    last = [[None] * PIECES for _ in range(4)]
    cross = [None] * PIECES
    part = edge * 2 // PIECES
    gather_count = [0]

    def gather_send(src, slot, p, peer):
        k = gather_count[0]
        gather_count[0] += 1
        return send(src, xall.at[slot, p], ag_s.at[k], ag_r.at[k], peer)

    def slot_of(side, shift):
        return side * ny + lax.rem(y + shift + ny, ny)

    def product(slot, ref=None):
        if ref is None:
            both = jnp.concatenate([xall[slot, p] for p in range(PIECES)], axis=1)
        else:
            both = jnp.concatenate([ref[:edge], ref[edge:]], axis=1)

        def some(q, carry):
            out = jnp.dot(
                tiles[slot, pl.ds(q * 4, 4)].reshape(4 * edge, edge), both, preferred_element_type=F32
            )
            at = slot * cap + q * 4
            prod[0, pl.ds(at, 4)] = out[:, :edge].reshape(4, edge, edge)
            prod[1, pl.ds(at, 4)] = out[:, edge:].reshape(4, edge, edge)
            return carry

        lax.fori_loop(0, cap // 4, some, 0)

    g_count = [0]
    near, seen = {}, set()
    sides = (xl, 1 - xl)

    def g_send(src, d, side, x_lo, peer):
        k = g_count[0]
        g_count[0] += 1
        near[d, side] = send(src, gall.at[reach + d, x_lo], g_s.at[k], g_r.at[k], peer)

    def g_wait(d, side):
        if (d, side) not in seen:
            seen.add((d, side))
            near[d, side].wait_recv()

    for step in range(yhalf):
        arrived = []
        for f, (side, way, steps) in enumerate(flows):
            which = xh if side == 0 else 1 - xh
            slot = slot_of(which, -way * step)
            if step > steps:
                continue
            for p in range(PIECES):
                src = xall.at[slot, p]
                if step == 0:
                    if side == 0:
                        src = x_ref.at[pl.ds(p * part, part)]
                    elif cross[p] is not None:
                        cross[p].wait_recv()
                        cross[p] = None
                else:
                    last[f][p].wait_recv()
                if step < steps:
                    last[f][p] = gather_send(src, slot, p, y_peer(way))
                if step == 0 and f == 0:
                    cross[p] = gather_send(src, row, p, partner)
                    if p == PIECES - 1:
                        g_send(g_ref, 0, 1, xl, x_peer)
                        if reach >= 1:
                            for zway in (1, -1):
                                g_send(g_ref, -zway, 0, xl, z_peer(zway))
            if step > 0:
                arrived.append(slot)
        if step == 0:
            for p in range(PIECES):
                if cross[p] is not None:
                    cross[p].wait_recv()
            product(row, x_ref)
            product((1 - xh) * ny + y)
        for slot in arrived:
            product(slot)
        if step == 1 or yhalf == 1:
            if reach >= 1:
                g_wait(0, 1)
                for zway in (1, -1):
                    g_send(gall.at[reach, 1 - xl], -zway, 1, 1 - xl, z_peer(zway))
        if step == 2 or (yhalf <= 2 and step == yhalf - 1):
            for hop in range(1, reach):
                for zway in (1, -1):
                    for side in range(2):
                        g_wait(-zway * hop, side)
                        g_send(
                            gall.at[reach - zway * hop, sides[side]],
                            -zway * (hop + 1), side, sides[side], z_peer(zway),
                        )
    for f, (side, way, steps) in enumerate(flows):
        if steps < yhalf:
            continue
        for p in range(PIECES):
            last[f][p].wait_recv()
        product(slot_of(xh if side == 0 else 1 - xh, -way * yhalf))

    for copy in to_scalar:
        copy.wait()

    def accumulate(k, run):
        code = codes[0, k]
        before = codes[0, jnp.maximum(k - 1, 0)]
        same = lax.div(code, 2 * slots) == lax.div(before, 2 * slots)
        run = prod[lax.rem(code, 2), lax.rem(lax.div(code, 2), slots)] + jnp.where(same, run, 0.0)
        runs[k] = run
        return run

    lax.fori_loop(0, slots, accumulate, jnp.zeros((edge, edge), F32), unroll=2)

    def tile_sum(t):
        upto = ends[0, t]
        below = jnp.where(t > 0, ends[0, jnp.maximum(t - 1, 0)], 0)
        return jnp.where(upto > below, runs[jnp.maximum(upto - 1, 0)], 0.0)

    def at_z(d):
        return lax.rem(z + d + nz, nz)

    order = [half]
    for d in range(half - 1, 0, -1):
        order += [d, -d]
    order.append(0)
    from_core = {}
    for k, d in enumerate(order):
        at = at_z(d)
        for side in range(XL):
            first = ((at * XL + side) * CORES + 1 - c) * 2
            for h in range(2):
                oth[at, side, h * edge : (h + 1) * edge] = tile_sum(first + h).astype(BF16)
        from_core[d] = send(oth.at[at], cbuf.at[at], c_s.at[k], c_r.at[k], core_peer)
    ready = set()

    def mine(d, side):
        if d == -half:
            d = half
        if d not in ready:
            from_core[d].wait_recv()
            ready.add(d)
        at = at_z(d)
        first = ((at * XL + side) * CORES + c) * 2
        own = jnp.concatenate([tile_sum(first), tile_sum(first + 1)], axis=0)
        return own + cbuf[at, side].astype(F32)

    def grad_term(m, g):
        high = m.astype(BF16)
        rest = m - high.astype(F32)
        middle = rest.astype(BF16)
        low = (rest - middle.astype(F32)).astype(BF16)
        total = None
        for v in (high, middle, low):
            term = lax.dot_general(v, g, (((0,), (0,)), ((), ())), preferred_element_type=F32)
            total = term if total is None else total + term
        return total

    def g_of(d, side):
        if (d, side) == (0, 0):
            return g_ref[...]
        g_wait(d, side)
        return gall[reach + d, sides[side]]

    side_a, side_b = 1 - xl, xl
    zflows = [(0, 1, half), (0, -1, half - 1), (1, 1, half - 1), (1, -1, half)]
    zlast = [None] * 4
    count = [0]

    def ring_step(distance, terms=None):
        for f, (side, way, steps) in enumerate(zflows):
            if distance > steps:
                continue
            total = mine(way * distance, side_a if side == 0 else side_b)
            if zlast[f] is not None:
                zlast[f][0].wait_recv()
                total = total + rbuf[zlast[f][1]].astype(F32)
            k = count[0]
            count[0] += 1
            sbuf[k] = total.astype(BF16)
            zlast[f] = (send(sbuf.at[k], rbuf.at[k], z_s.at[k], z_r.at[k], z_peer(way)), k)
            if terms is not None:
                mbuf[terms + f] = total

    def ring_end(side, first, second):
        total = mine(0, side)
        for f in (first, second):
            if zlast[f] is not None:
                zlast[f][0].wait_recv()
                total = total + rbuf[zlast[f][1]].astype(F32)
        return total

    for distance in range(half, reach, -1):
        ring_step(distance)
    if reach >= 1:
        inner = None
        for d in range(1 - reach, reach):
            for s_i, side in ((1, side_a), (0, side_b)):
                term = grad_term(mine(d, side), g_of(d, s_i))
                inner = term if inner is None else inner + term
        gbuf[...] = inner
        ring_step(reach, 0)
        outer = gbuf[...]
        for f, (side, way, steps) in enumerate(zflows):
            outer = outer + grad_term(mbuf[f], g_of(way * reach, 1 if side == 0 else 0))
        gbuf[...] = outer
    else:
        xsend[...] = ring_end(side_a, 0, 1)
        over = send(xsend, xrecv, x_s, x_r, x_peer)
        mbuf[0] = ring_end(side_b, 2, 3)
        gbuf[...] = grad_term(xsend[...], g_of(0, 1)) + grad_term(mbuf[0], g_of(0, 0))

    used = [0]

    def pair():
        k = used[0]
        used[0] += 1
        return a_s.at[k], a_r.at[k]

    def total_of(slots_ref, m):
        total = slots_ref[0]
        for k in range(1, m):
            total = total + slots_ref[k]
        return total

    hrows = gbuf.shape[0] // 2
    here = pl.ds(pl.multiple_of(c * hrows, hrows), hrows)
    there = pl.ds(pl.multiple_of((1 - c) * hrows, hrows), hrows)
    first = send(gbuf.at[there], r1, *pair(), core_peer)
    first.wait_recv()
    hbuf[...] = (gbuf[here] + r1[...]).reshape(hbuf.shape)
    r2[y] = hbuf[y]
    over_y = [send(hbuf.at[lax.rem(y + d, ny)], r2.at[y], *pair(), y_peer(d)) for d in range(1, ny)]
    for distance in range(reach - 1, 0, -1):
        ring_step(distance)
    for copy in over_y:
        copy.wait_recv()
    vbuf[...] = total_of(r2, ny)
    r3[x] = vbuf[...]
    over_x = [send(vbuf, r3.at[x], *pair(), x4_peer(d)) for d in range(1, 4)]
    if reach >= 1:
        xsend[...] = ring_end(side_a, 0, 1)
        over = send(xsend, xrecv, x_s, x_r, x_peer)
        mbuf[0] = ring_end(side_b, 2, 3)
    for copy in over_x:
        copy.wait_recv()
    ubuf[...] = total_of(r3, 4)
    r4[z] = ubuf[...]
    over_z = [send(ubuf, r4.at[z], *pair(), z_peer(d)) for d in range(1, nz)]
    over.wait_recv()
    aggregate = mbuf[0] + xrecv[...]
    mixed_ref[...] = jnp.dot(
        aggregate.astype(BF16), w_ref[...], preferred_element_type=F32
    ).astype(BF16)
    for copy in over_z:
        copy.wait_recv()
    tbuf[...] = total_of(r4, nz)
    r5[y] = tbuf[...]
    back = [send(tbuf, r5.at[y], *pair(), y_peer(d)) for d in range(1, ny)]
    other = [send(tbuf, r6.at[y], *pair(), core_peer)]
    for d, copy in enumerate(back):
        copy.wait_recv()
        at = lax.rem(y - (d + 1) + ny, ny)
        other.append(send(r5.at[at], r6.at[at], *pair(), core_peer))
    for copy in other:
        copy.wait_recv()
    grad_ref[here] = r5[...].reshape(hrows, -1)
    grad_ref[there] = r6[...].reshape(hrows, -1)
    for copy in started:
        copy.wait_send()


def body(node_features, layer_weight, tile_values, tile_positions, section_tile_count, out_cotangent):
    sections, cap, edge, _ = tile_values.shape[1:]
    ny = sections // XH
    nz = lax.axis_size("rep") // (XL * CORES)
    reach = min(2, nz // 2 - 1)
    slots = sections * cap
    f, h = layer_weight.shape
    rows = out_cotangent.shape[0]
    copies = 2 * (nz - 1)
    gathers = PIECES * (1 + 2 * (ny - 1))
    g_copies = 1 + 4 * reach
    hrows = f // 2
    piece = hrows // ny
    small = 1 + 2 * (ny - 1) + 3 + (nz - 1) + ny
    width = max(128, nz * 8)
    dma, vmem, smem = pltpu.SemaphoreType.DMA, pltpu.VMEM, pltpu.SMEM
    whole = pl.BlockSpec(memory_space=pltpu.VMEM)
    return pl.pallas_call(
        functools.partial(kernel, ny, nz, reach),
        out_shape=(
            jax.ShapeDtypeStruct((rows, h), BF16),
            jax.ShapeDtypeStruct((f, h), F32),
        ),
        in_specs=[whole, whole, pl.BlockSpec(memory_space=pl.ANY), whole, whole, whole],
        out_specs=(whole, whole),
        scratch_shapes=[
            vmem((sections, cap, edge, edge), BF16),
            vmem((sections, PIECES, rows // PIECES, f), BF16),
            vmem((2, slots, edge, f), F32),
            vmem((slots, edge, f), F32),
            vmem((1, slots), I32),
            vmem((1, width), I32),
            smem((1, slots), I32),
            smem((1, width), I32),
            vmem((2 * reach + 1, XL, rows, h), BF16),
            vmem((nz, XL, rows, f), BF16),
            vmem((nz, XL, rows, f), BF16),
            vmem((copies, rows, f), BF16),
            vmem((copies, rows, f), BF16),
            vmem((4, rows, f), F32),
            vmem((rows, f), F32),
            vmem((rows, f), F32),
            vmem((f, h), F32),
            vmem((hrows, h), F32),
            vmem((ny, piece, h), F32),
            vmem((ny, piece, h), F32),
            vmem((piece, h), F32),
            vmem((4, piece, h), F32),
            vmem((piece, h), F32),
            vmem((nz, piece, h), F32),
            vmem((piece, h), F32),
            vmem((ny, piece, h), F32),
            vmem((ny, piece, h), F32),
            dma, dma((2,)), dma((gathers,)), dma((gathers,)), dma((g_copies,)), dma((g_copies,)),
            dma((nz,)), dma((nz,)), dma((copies,)), dma((copies,)), dma, dma, dma((small,)), dma((small,)),
        ],
        compiler_params=pltpu.CompilerParams(
            collective_id=0, has_side_effects=True, vmem_limit_bytes=56 << 20
        ),
        name="graph_layer",
    )(node_features, layer_weight, tile_values[0], tile_positions, section_tile_count, out_cotangent)


def solution(mesh):
    placed = (
        P(("row", "rep"), None),
        P(),
        P("row", "rep", None, None, None),
        P("row", "rep", None),
        P("row", "rep"),
        P(("row", "rep"), None),
    )
    return jax.shard_map(
        body, mesh=mesh, in_specs=placed, out_specs=(P(("row", "rep"), None), P()), check_vma=False
    )
```

```python
import functools

import jax
import jax.numpy as jnp
from jax import lax
from jax.experimental import pallas as pl
from jax.experimental.pallas import tpu as pltpu
from jax.sharding import PartitionSpec as P

MESH = pl.DeviceIdType.MESH
F32, BF16, I32 = jnp.float32, jnp.bfloat16, jnp.int32
XH, XL, CORES = 2, 2, 2
PIECES = 2


def iota(shape, dim):
    return lax.broadcasted_iota(I32, shape, dim)


def sort_slots(pos, cnt, tiles_all, width):
    n, cap = pos.shape
    slots = n * cap
    diag = iota((n, n), 0) == iota((n, n), 1)
    count = jnp.sum(jnp.where(diag, jnp.broadcast_to(cnt, (n, n)), 0), axis=1, keepdims=True)
    slot = iota((n, cap), 1)
    key = jnp.where(slot < count, lax.div(pos, 2), tiles_all)
    code = (key * slots + iota((n, cap), 0) * cap + slot) * 2 + lax.rem(pos, 2)
    spread = jnp.broadcast_to(code[:, None, :], (n, cap, cap))
    picked = jnp.where(iota((n, cap, cap), 1) == iota((n, cap, cap), 2), spread, 0)
    column = jnp.sum(picked, axis=2, keepdims=True).reshape(slots, 1)
    grid = jnp.broadcast_to(column, (slots, slots))
    lane = iota((slots, slots), 1)
    line = jnp.sum(jnp.where(iota((slots, slots), 0) == lane, grid, 0), axis=0, keepdims=True)
    rank = jnp.sum(jnp.where(line < grid, 1, 0), axis=1, keepdims=True)
    ordered = jnp.sum(jnp.where(rank == lane, grid, 0), axis=0, keepdims=True)
    rows = lax.div(jnp.broadcast_to(column, (slots, width)), 2 * slots)
    ends = jnp.sum(jnp.where(rows <= iota((slots, width), 1), 1, 0), axis=0, keepdims=True)
    return ordered, ends


def kernel(
    ny, nz, reach, x_ref, w_ref, tile_ref, pos_ref, cnt_ref, g_ref, mixed_ref, grad_ref,
    tiles, xall, prod, runs, codes_v, ends_v, codes, ends, gall, oth, cbuf, sbuf, rbuf, mbuf,
    xsend, xrecv, gbuf, r1, hbuf, r2, vbuf, r3, ubuf, r4, tbuf, r5, r6,
    t_s, i_s, ag_s, ag_r, g_s, g_r, c_s, c_r, z_s, z_r, x_s, x_r, a_s, a_r,
):
    row, rep = lax.axis_index("row"), lax.axis_index("rep")
    xh, y = row // ny, lax.rem(row, ny)
    z, xl, c = rep // 4, lax.rem(rep // 2, 2), lax.rem(rep, 2)
    x = xh * 2 + xl
    half, yhalf = nz // 2, ny // 2
    n, cap, edge = tiles.shape[0], tiles.shape[1], tiles.shape[2]
    slots = n * cap

    partner = ((1 - xh) * ny + y, rep)
    core_peer = (row, rep + 1 - 2 * c)
    x_peer = (row, z * 4 + (1 - xl) * 2 + c)

    def z_peer(d):
        return (row, lax.rem(z + d + nz, nz) * 4 + xl * 2 + c)

    def y_peer(d):
        return (xh * ny + lax.rem(y + d + ny, ny), rep)

    def x4_peer(d):
        q = lax.rem(x + d, 4)
        return ((q // 2) * ny + y, z * 4 + lax.rem(q, 2) * 2 + c)

    started = []

    def send(src, dst, s_sem, r_sem, peer):
        copy = pltpu.make_async_remote_copy(src, dst, s_sem, r_sem, device_id=peer, device_id_type=MESH)
        copy.start()
        started.append(copy)
        return copy

    load_tiles = pltpu.make_async_copy(tile_ref, tiles, t_s)
    load_tiles.start()
    barrier = pltpu.get_barrier_semaphore()
    peers = [partner, core_peer, x_peer, z_peer(1), y_peer(1)]
    if nz > 2:
        peers.append(z_peer(-1))
    if ny > 2:
        peers.append(y_peer(-1))
    for peer in peers:
        pl.semaphore_signal(barrier, inc=1, device_id=peer, device_id_type=MESH)
    pl.semaphore_wait(barrier, len(peers))

    part = edge * 2 // PIECES
    gather_count = [0]

    def gather_send(src, slot, p, peer):
        k = gather_count[0]
        gather_count[0] += 1
        return send(src, xall.at[slot, p], ag_s.at[k], ag_r.at[k], peer)

    def slot_of(side, shift):
        return side * ny + lax.rem(y + shift + ny, ny)

    def product(slot, ref=None):
        if ref is None:
            both = jnp.concatenate([xall[slot, p] for p in range(PIECES)], axis=1)
        else:
            both = jnp.concatenate([ref[:edge], ref[edge:]], axis=1)

        def some(q, carry):
            out = jnp.dot(
                tiles[slot, pl.ds(q * 4, 4)].reshape(4 * edge, edge), both, preferred_element_type=F32
            )
            at = slot * cap + q * 4
            prod[0, pl.ds(at, 4)] = out[:, :edge].reshape(4, edge, edge)
            prod[1, pl.ds(at, 4)] = out[:, edge:].reshape(4, edge, edge)
            return carry

        lax.fori_loop(0, cap // 4, some, 0)

    g_count = [0]
    near, seen = {}, set()
    sides = (xl, 1 - xl)

    def g_send(src, d, side, x_lo, peer):
        k = g_count[0]
        g_count[0] += 1
        near[d, side] = send(src, gall.at[reach + d, x_lo], g_s.at[k], g_r.at[k], peer)

    def g_wait(d, side):
        if (d, side) not in seen:
            seen.add((d, side))
            near[d, side].wait_recv()

    bound = yhalf // 2
    chains, over = {}, {}

    def steps_of(side, way, p):
        if side == 1:
            return bound
        return yhalf if (way == 1) == (p == 0) else yhalf - 1

    def forward(side, way, p, distance):
        slot = slot_of(xh if side == 0 else 1 - xh, -way * distance)
        src = xall.at[slot, p]
        if distance == 0 and side == 0:
            src = x_ref.at[pl.ds(p * part, part)]
        elif distance > 0:
            chains[side, way, p].wait_recv()
        if distance < steps_of(side, way, p):
            chains[side, way, p] = gather_send(src, slot, p, y_peer(way))
        if side == 0 and distance > bound:
            over[way, p, distance] = gather_send(src, slot, p, partner)

    def from_partner(distance):
        for way in (1, -1):
            for p in range(PIECES):
                if distance <= steps_of(0, way, p):
                    over[way, p, distance].wait_recv()
        for way in (1, -1) if distance < yhalf else (1,):
            product(slot_of(1 - xh, -way * distance))

    def send_g(hop):
        for zway in (1, -1):
            for side in range(2):
                g_wait(-zway * hop, side)
                g_send(
                    gall.at[reach - zway * hop, sides[side]],
                    -zway * (hop + 1), side, sides[side], z_peer(zway),
                )

    for p in range(PIECES):
        for way in (1, -1):
            forward(0, way, p, 0)
        over[0, p, 0] = gather_send(x_ref.at[pl.ds(p * part, part)], row, p, partner)
    g_send(g_ref, 0, 1, xl, x_peer)
    if reach >= 1:
        for zway in (1, -1):
            g_send(g_ref, -zway, 0, xl, z_peer(zway))
    tiles_all = nz * 8
    codes_v[...], ends_v[...] = sort_slots(pos_ref[0], cnt_ref[...], tiles_all, ends_v.shape[1])
    to_scalar = [pltpu.make_async_copy(codes_v, codes, i_s.at[0]), pltpu.make_async_copy(ends_v, ends, i_s.at[1])]
    for copy in to_scalar:
        copy.start()
    load_tiles.wait()
    product(row, x_ref)
    for p in range(PIECES):
        over[0, p, 0].wait_recv()
        if bound > 0:
            for way in (1, -1):
                forward(1, way, p, 0)
    product((1 - xh) * ny + y)
    for distance in range(1, yhalf + 1):
        for p in range(PIECES):
            for way in (1, -1):
                if distance <= steps_of(0, way, p):
                    forward(0, way, p, distance)
        if distance <= bound:
            for p in range(PIECES):
                for way in (1, -1):
                    forward(1, way, p, distance)
        for way in (1, -1) if distance < yhalf else (1,):
            product(slot_of(xh, -way * distance))
        if distance <= bound:
            for way in (1, -1):
                product(slot_of(1 - xh, -way * distance))
        if distance - 1 > bound:
            from_partner(distance - 1)
        if distance == 1 and reach >= 1:
            g_wait(0, 1)
            for zway in (1, -1):
                g_send(gall.at[reach, 1 - xl], -zway, 1, 1 - xl, z_peer(zway))
        for hop in range(1, reach):
            if distance == min(hop + 1, yhalf):
                send_g(hop)
    from_partner(yhalf)

    for copy in to_scalar:
        copy.wait()

    def accumulate(k, run):
        code = codes[0, k]
        before = codes[0, jnp.maximum(k - 1, 0)]
        same = lax.div(code, 2 * slots) == lax.div(before, 2 * slots)
        run = prod[lax.rem(code, 2), lax.rem(lax.div(code, 2), slots)] + jnp.where(same, run, 0.0)
        runs[k] = run
        return run

    lax.fori_loop(0, slots, accumulate, jnp.zeros((edge, edge), F32), unroll=2)

    def tile_sum(t):
        upto = ends[0, t]
        below = jnp.where(t > 0, ends[0, jnp.maximum(t - 1, 0)], 0)
        return jnp.where(upto > below, runs[jnp.maximum(upto - 1, 0)], 0.0)

    def at_z(d):
        return lax.rem(z + d + nz, nz)

    order = [half]
    for d in range(half - 1, 0, -1):
        order += [d, -d]
    order.append(0)
    from_core, ready = {}, set()

    def emit(d):
        at = at_z(d)
        for side in range(XL):
            first = ((at * XL + side) * CORES + 1 - c) * 2
            for h in range(2):
                oth[at, side, h] = tile_sum(first + h).astype(BF16)
        k = len(from_core)
        from_core[d] = send(oth.at[at], cbuf.at[at], c_s.at[k], c_r.at[k], core_peer)

    pending = list(order)

    def emit_some(m):
        for _ in range(m):
            if pending:
                emit(pending.pop(0))

    def mine(d, side, h):
        if d == -half:
            d = half
        if d not in ready:
            from_core[d].wait_recv()
            ready.add(d)
        at = at_z(d)
        return tile_sum(((at * XL + side) * CORES + c) * 2 + h) + cbuf[at, side, h].astype(F32)

    def mine_both(d, side):
        return jnp.concatenate([mine(d, side, 0), mine(d, side, 1)], axis=0)

    def grad_term(m, g):
        high = m.astype(BF16)
        low = (m - high.astype(F32)).astype(BF16)
        total = None
        for v in (high, low):
            term = lax.dot_general(v, g, (((0,), (0,)), ((), ())), preferred_element_type=F32)
            total = term if total is None else total + term
        return total

    def g_of(d, side):
        if (d, side) == (0, 0):
            return g_ref[...]
        g_wait(d, side)
        return gall[reach + d, sides[side]]

    side_a, side_b = 1 - xl, xl
    zflows = [(0, 1, half), (0, -1, half - 1), (1, 1, half - 1), (1, -1, half)]
    zlast = {}
    count = [0]

    def ring_step(distance, terms=False):
        for f, (side, way, steps) in enumerate(zflows):
            if distance > steps:
                continue
            for h in range(2):
                total = mine(way * distance, side_a if side == 0 else side_b, h)
                if (f, h) in zlast:
                    zlast[f, h][0].wait_recv()
                    total = total + rbuf[zlast[f, h][1]].astype(F32)
                k = count[0]
                count[0] += 1
                sbuf[k] = total.astype(BF16)
                zlast[f, h] = (send(sbuf.at[k], rbuf.at[k], z_s.at[k], z_r.at[k], z_peer(way)), k)
                if terms:
                    mbuf[h * edge : (h + 1) * edge] = total
            if terms:
                gbuf[...] += grad_term(mbuf[...], g_of(way * reach, 1 if side == 0 else 0))

    def ring_end(side, first, second, out):
        for h in range(2):
            total = mine(0, side, h)
            for f in (first, second):
                if (f, h) in zlast:
                    zlast[f, h][0].wait_recv()
                    total = total + rbuf[zlast[f, h][1]].astype(F32)
            out[h * edge : (h + 1) * edge] = total

    def inner_terms(distances):
        for d in distances:
            gbuf[...] += grad_term(mine_both(d, side_a), g_of(d, 1))
            gbuf[...] += grad_term(mine_both(d, side_b), g_of(d, 0))

    gbuf[...] = jnp.zeros_like(gbuf)
    inner = sorted(range(1 - reach, reach), key=abs, reverse=True)
    emit_some(3)
    for distance in range(half, reach, -1):
        ring_step(distance)
        emit_some(len(pending) if distance <= reach + 2 else 4)
        if distance == reach + 2:
            inner_terms(inner[: reach - 1])
            inner = inner[reach - 1 :]
    emit_some(len(pending))
    if reach >= 1:
        inner_terms(inner)
        ring_step(reach, True)
    else:
        ring_end(side_a, 0, 1, xsend)
        over_x_pair = send(xsend, xrecv, x_s, x_r, x_peer)
        ring_end(side_b, 2, 3, mbuf)
        gbuf[...] = grad_term(xsend[...], g_of(0, 1)) + grad_term(mbuf[...], g_of(0, 0))

    used = [0]

    def pair():
        k = used[0]
        used[0] += 1
        return a_s.at[k], a_r.at[k]

    def total_of(slots_ref, m):
        total = slots_ref[0]
        for k in range(1, m):
            total = total + slots_ref[k]
        return total

    hrows = gbuf.shape[0] // 2
    here = pl.ds(pl.multiple_of(c * hrows, hrows), hrows)
    there = pl.ds(pl.multiple_of((1 - c) * hrows, hrows), hrows)
    first = send(gbuf.at[there], r1, *pair(), core_peer)
    first.wait_recv()
    hbuf[...] = (gbuf[here] + r1[...]).reshape(hbuf.shape)
    r2[y] = hbuf[y]
    over_y = [send(hbuf.at[lax.rem(y + d, ny)], r2.at[y], *pair(), y_peer(d)) for d in range(1, ny)]
    for distance in range(reach - 1, 0, -1):
        ring_step(distance)
    for copy in over_y:
        copy.wait_recv()
    vbuf[...] = total_of(r2, ny)
    r3[x] = vbuf[...]
    over_x = [send(vbuf, r3.at[x], *pair(), x4_peer(d)) for d in range(1, 4)]
    if reach >= 1:
        ring_end(side_a, 0, 1, xsend)
        over_x_pair = send(xsend, xrecv, x_s, x_r, x_peer)
        ring_end(side_b, 2, 3, mbuf)
    for copy in over_x:
        copy.wait_recv()
    ubuf[...] = total_of(r3, 4)
    r4[z] = ubuf[...]
    over_z = [send(ubuf, r4.at[z], *pair(), z_peer(d)) for d in range(1, nz)]
    over_x_pair.wait_recv()
    aggregate = mbuf[...] + xrecv[...]
    mixed_ref[...] = jnp.dot(
        aggregate.astype(BF16), w_ref[...], preferred_element_type=F32
    ).astype(BF16)
    for copy in over_z:
        copy.wait_recv()
    tbuf[...] = total_of(r4, nz)
    r5[y] = tbuf[...]
    back = [send(tbuf, r5.at[y], *pair(), y_peer(d)) for d in range(1, ny)]
    other = [send(tbuf, r6.at[y], *pair(), core_peer)]
    for d, copy in enumerate(back):
        copy.wait_recv()
        at = lax.rem(y - (d + 1) + ny, ny)
        other.append(send(r5.at[at], r6.at[at], *pair(), core_peer))
    for copy in other:
        copy.wait_recv()
    grad_ref[here] = r5[...].reshape(hrows, -1)
    grad_ref[there] = r6[...].reshape(hrows, -1)
    for copy in started:
        copy.wait_send()


def body(node_features, layer_weight, tile_values, tile_positions, section_tile_count, out_cotangent):
    sections, cap, edge, _ = tile_values.shape[1:]
    ny = sections // XH
    nz = lax.axis_size("rep") // (XL * CORES)
    reach = min(3, nz // 2 - 1)
    slots = sections * cap
    f, h = layer_weight.shape
    rows = out_cotangent.shape[0]
    copies = 4 * (nz - 1)
    gathers = PIECES * (1 + 2 * (ny - 1))
    g_copies = 1 + 4 * reach
    hrows = f // 2
    piece = hrows // ny
    small = 1 + 2 * (ny - 1) + 3 + (nz - 1) + ny
    width = max(128, nz * 8)
    dma, vmem, smem = pltpu.SemaphoreType.DMA, pltpu.VMEM, pltpu.SMEM
    whole = pl.BlockSpec(memory_space=pltpu.VMEM)
    return pl.pallas_call(
        functools.partial(kernel, ny, nz, reach),
        out_shape=(
            jax.ShapeDtypeStruct((rows, h), BF16),
            jax.ShapeDtypeStruct((f, h), F32),
        ),
        in_specs=[whole, whole, pl.BlockSpec(memory_space=pl.ANY), whole, whole, whole],
        out_specs=(whole, whole),
        scratch_shapes=[
            vmem((sections, cap, edge, edge), BF16),
            vmem((sections, PIECES, rows // PIECES, f), BF16),
            vmem((2, slots, edge, f), F32),
            vmem((slots, edge, f), F32),
            vmem((1, slots), I32),
            vmem((1, width), I32),
            smem((1, slots), I32),
            smem((1, width), I32),
            vmem((2 * reach + 1, XL, rows, h), BF16),
            vmem((nz, XL, 2, edge, f), BF16),
            vmem((nz, XL, 2, edge, f), BF16),
            vmem((copies, edge, f), BF16),
            vmem((copies, edge, f), BF16),
            vmem((rows, f), F32),
            vmem((rows, f), F32),
            vmem((rows, f), F32),
            vmem((f, h), F32),
            vmem((hrows, h), F32),
            vmem((ny, piece, h), F32),
            vmem((ny, piece, h), F32),
            vmem((piece, h), F32),
            vmem((4, piece, h), F32),
            vmem((piece, h), F32),
            vmem((nz, piece, h), F32),
            vmem((piece, h), F32),
            vmem((ny, piece, h), F32),
            vmem((ny, piece, h), F32),
            dma, dma((2,)), dma((gathers,)), dma((gathers,)), dma((g_copies,)), dma((g_copies,)),
            dma((nz,)), dma((nz,)), dma((copies,)), dma((copies,)), dma, dma, dma((small,)), dma((small,)),
        ],
        compiler_params=pltpu.CompilerParams(
            collective_id=0, has_side_effects=True, vmem_limit_bytes=56 << 20
        ),
        name="graph_layer",
    )(node_features, layer_weight, tile_values[0], tile_positions, section_tile_count, out_cotangent)


def solution(mesh):
    placed = (
        P(("row", "rep"), None),
        P(),
        P("row", "rep", None, None, None),
        P("row", "rep", None),
        P("row", "rep"),
        P(("row", "rep"), None),
    )
    return jax.shard_map(
        body, mesh=mesh, in_specs=placed, out_specs=(P(("row", "rep"), None), P()), check_vma=False
    )
```

```python
import functools

import jax
import jax.numpy as jnp
from jax import lax
from jax.experimental import pallas as pl
from jax.experimental.pallas import tpu as pltpu
from jax.sharding import PartitionSpec as P

MESH = pl.DeviceIdType.MESH
F32, BF16, I32 = jnp.float32, jnp.bfloat16, jnp.int32
XH, XL, CORES = 2, 2, 2
PIECES = 2


def iota(shape, dim):
    return lax.broadcasted_iota(I32, shape, dim)


def sort_slots(pos, cnt, tiles_all, width):
    n, cap = pos.shape
    slots = n * cap
    diag = iota((n, n), 0) == iota((n, n), 1)
    count = jnp.sum(jnp.where(diag, jnp.broadcast_to(cnt, (n, n)), 0), axis=1, keepdims=True)
    slot = iota((n, cap), 1)
    key = jnp.where(slot < count, lax.div(pos, 2), tiles_all)
    code = (key * slots + iota((n, cap), 0) * cap + slot) * 2 + lax.rem(pos, 2)
    spread = jnp.broadcast_to(code[:, None, :], (n, cap, cap))
    picked = jnp.where(iota((n, cap, cap), 1) == iota((n, cap, cap), 2), spread, 0)
    column = jnp.sum(picked, axis=2, keepdims=True).reshape(slots, 1)
    grid = jnp.broadcast_to(column, (slots, slots))
    lane = iota((slots, slots), 1)
    line = jnp.sum(jnp.where(iota((slots, slots), 0) == lane, grid, 0), axis=0, keepdims=True)
    rank = jnp.sum(jnp.where(line < grid, 1, 0), axis=1, keepdims=True)
    ordered = jnp.sum(jnp.where(rank == lane, grid, 0), axis=0, keepdims=True)
    rows = lax.div(jnp.broadcast_to(column, (slots, width)), 2 * slots)
    ends = jnp.sum(jnp.where(rows <= iota((slots, width), 1), 1, 0), axis=0, keepdims=True)
    return ordered, ends


def kernel(
    ny, nz, reach, x_ref, w_ref, tile_ref, pos_ref, cnt_ref, g_ref, mixed_ref, grad_ref,
    tiles, xall, prod, runs, codes_v, ends_v, codes, ends, gall, oth, cbuf, sbuf, rbuf, mbuf,
    xsend, xrecv, gbuf, r1, hbuf, r2, vbuf, r3, ubuf, r4, tbuf, r5, r6,
    t_s, i_s, ag_s, ag_r, g_s, g_r, c_s, c_r, z_s, z_r, x_s, x_r, a_s, a_r,
):
    row, rep = lax.axis_index("row"), lax.axis_index("rep")
    xh, y = row // ny, lax.rem(row, ny)
    z, xl, c = rep // 4, lax.rem(rep // 2, 2), lax.rem(rep, 2)
    x = xh * 2 + xl
    half, yhalf = nz // 2, ny // 2
    n, cap, edge = tiles.shape[0], tiles.shape[1], tiles.shape[2]
    slots = n * cap

    partner = ((1 - xh) * ny + y, rep)
    core_peer = (row, rep + 1 - 2 * c)
    x_peer = (row, z * 4 + (1 - xl) * 2 + c)

    def z_peer(d):
        return (row, lax.rem(z + d + nz, nz) * 4 + xl * 2 + c)

    def y_peer(d):
        return (xh * ny + lax.rem(y + d + ny, ny), rep)

    def x4_peer(d):
        q = lax.rem(x + d, 4)
        return ((q // 2) * ny + y, z * 4 + lax.rem(q, 2) * 2 + c)

    started = []

    def send(src, dst, s_sem, r_sem, peer):
        copy = pltpu.make_async_remote_copy(src, dst, s_sem, r_sem, device_id=peer, device_id_type=MESH)
        copy.start()
        started.append(copy)
        return copy

    load_tiles = pltpu.make_async_copy(tile_ref, tiles, t_s)
    load_tiles.start()
    barrier = pltpu.get_barrier_semaphore()
    peers = [partner, core_peer, x_peer, z_peer(1), y_peer(1)]
    if nz > 2:
        peers.append(z_peer(-1))
    if ny > 2:
        peers.append(y_peer(-1))
    for peer in peers:
        pl.semaphore_signal(barrier, inc=1, device_id=peer, device_id_type=MESH)
    tiles_all = nz * 8
    codes_v[...], ends_v[...] = sort_slots(pos_ref[0], cnt_ref[...], tiles_all, ends_v.shape[1])
    to_scalar = [pltpu.make_async_copy(codes_v, codes, i_s.at[0]), pltpu.make_async_copy(ends_v, ends, i_s.at[1])]
    for copy in to_scalar:
        copy.start()
    pl.semaphore_wait(barrier, len(peers))

    part = edge * 2 // PIECES
    gather_count = [0]

    def gather_send(src, slot, p, peer):
        k = gather_count[0]
        gather_count[0] += 1
        return send(src, xall.at[slot, p], ag_s.at[k], ag_r.at[k], peer)

    def slot_of(side, shift):
        return side * ny + lax.rem(y + shift + ny, ny)

    def product(slot, ref=None):
        if ref is None:
            both = jnp.concatenate([xall[slot, p] for p in range(PIECES)], axis=1)
        else:
            both = jnp.concatenate([ref[:edge], ref[edge:]], axis=1)

        def some(q, carry):
            out = jnp.dot(
                tiles[slot, pl.ds(q * 4, 4)].reshape(4 * edge, edge), both, preferred_element_type=F32
            )
            at = slot * cap + q * 4
            prod[0, pl.ds(at, 4)] = out[:, :edge].reshape(4, edge, edge)
            prod[1, pl.ds(at, 4)] = out[:, edge:].reshape(4, edge, edge)
            return carry

        lax.fori_loop(0, cap // 4, some, 0)

    g_count = [0]
    near, seen = {}, set()
    sides = (xl, 1 - xl)

    def g_send(src, d, side, x_lo, peer):
        k = g_count[0]
        g_count[0] += 1
        near[d, side] = send(src, gall.at[reach + d, x_lo], g_s.at[k], g_r.at[k], peer)

    def g_wait(d, side):
        if (d, side) not in seen:
            seen.add((d, side))
            near[d, side].wait_recv()

    chains, over = {}, {}

    def steps_of(side, way, p):
        return yhalf if ((way == 1) == (p == 0)) == (side == 0) else yhalf - 1

    def forward(side, way, p, distance):
        slot = slot_of(xh if side == 0 else 1 - xh, -way * distance)
        src = xall.at[slot, p]
        if distance == 0 and side == 0:
            src = x_ref.at[pl.ds(p * part, part)]
        elif distance > 0:
            chains[side, way, p].wait_recv()
        if distance < steps_of(side, way, p):
            chains[side, way, p] = gather_send(src, slot, p, y_peer(way))

    def send_g(hop):
        for zway in (1, -1):
            for side in range(2):
                g_wait(-zway * hop, side)
                g_send(
                    gall.at[reach - zway * hop, sides[side]],
                    -zway * (hop + 1), side, sides[side], z_peer(zway),
                )

    for p in range(PIECES):
        for way in (1, -1):
            forward(0, way, p, 0)
        over[p] = gather_send(x_ref.at[pl.ds(p * part, part)], row, p, partner)
    g_send(g_ref, 0, 1, xl, x_peer)
    if reach >= 1:
        for zway in (1, -1):
            g_send(g_ref, -zway, 0, xl, z_peer(zway))
    for p in range(PIECES):
        over[p].wait_recv()
        for way in (1, -1):
            forward(1, way, p, 0)
    load_tiles.wait()
    product(row, x_ref)
    product((1 - xh) * ny + y)
    for distance in range(1, yhalf + 1):
        ways = (1, -1) if distance < yhalf else (1,)
        for side in range(2):
            for p in range(PIECES):
                for way in (1, -1):
                    if distance <= steps_of(side, way, p):
                        forward(side, way, p, distance)
        for side in range(2):
            for way in ways:
                product(slot_of(xh if side == 0 else 1 - xh, -way * distance))
        if distance == 1 and reach >= 1:
            g_wait(0, 1)
            for zway in (1, -1):
                g_send(gall.at[reach, 1 - xl], -zway, 1, 1 - xl, z_peer(zway))
    for hop in range(1, reach):
        send_g(hop)

    for copy in to_scalar:
        copy.wait()

    def accumulate(k, run):
        code = codes[0, k]
        before = codes[0, jnp.maximum(k - 1, 0)]
        same = lax.div(code, 2 * slots) == lax.div(before, 2 * slots)
        run = prod[lax.rem(code, 2), lax.rem(lax.div(code, 2), slots)] + jnp.where(same, run, 0.0)
        runs[k] = run
        return run

    lax.fori_loop(0, slots, accumulate, jnp.zeros((edge, edge), F32), unroll=2)

    def tile_sum(t):
        upto = ends[0, t]
        below = jnp.where(t > 0, ends[0, jnp.maximum(t - 1, 0)], 0)
        return jnp.where(upto > below, runs[jnp.maximum(upto - 1, 0)], 0.0)

    def at_z(d):
        return lax.rem(z + d + nz, nz)

    order = [half]
    for d in range(half - 1, 0, -1):
        order += [d, -d]
    order.append(0)
    from_core, ready = {}, set()

    def emit(d):
        at = at_z(d)
        for side in range(XL):
            first = ((at * XL + side) * CORES + 1 - c) * 2
            for h in range(2):
                oth[at, side, h] = tile_sum(first + h).astype(BF16)
        k = len(from_core)
        from_core[d] = send(oth.at[at], cbuf.at[at], c_s.at[k], c_r.at[k], core_peer)

    pending = list(order)

    def emit_some(m):
        for _ in range(m):
            if pending:
                emit(pending.pop(0))

    def mine(d, side, h):
        if d == -half:
            d = half
        if d not in ready:
            from_core[d].wait_recv()
            ready.add(d)
        at = at_z(d)
        return tile_sum(((at * XL + side) * CORES + c) * 2 + h) + cbuf[at, side, h].astype(F32)

    def mine_both(d, side):
        return jnp.concatenate([mine(d, side, 0), mine(d, side, 1)], axis=0)

    def grad_term(m, g):
        high = m.astype(BF16)
        low = (m - high.astype(F32)).astype(BF16)
        total = None
        for v in (high, low):
            term = lax.dot_general(v, g, (((0,), (0,)), ((), ())), preferred_element_type=F32)
            total = term if total is None else total + term
        return total

    def g_of(d, side):
        if (d, side) == (0, 0):
            return g_ref[...]
        g_wait(d, side)
        return gall[reach + d, sides[side]]

    side_a, side_b = 1 - xl, xl
    zflows = [(0, 1, half), (0, -1, half - 1), (1, 1, half - 1), (1, -1, half)]
    zlast = {}
    count = [0]

    def ring_step(distance, terms=False):
        for f, (side, way, steps) in enumerate(zflows):
            if distance > steps:
                continue
            for h in range(2):
                total = mine(way * distance, side_a if side == 0 else side_b, h)
                if (f, h) in zlast:
                    zlast[f, h][0].wait_recv()
                    total = total + rbuf[zlast[f, h][1]].astype(F32)
                k = count[0]
                count[0] += 1
                sbuf[k] = total.astype(BF16)
                zlast[f, h] = (send(sbuf.at[k], rbuf.at[k], z_s.at[k], z_r.at[k], z_peer(way)), k)
                if terms:
                    mbuf[h * edge : (h + 1) * edge] = total
            if terms:
                gbuf[...] += grad_term(mbuf[...], g_of(way * reach, 1 if side == 0 else 0))

    def ring_end(side, first, second, out):
        for h in range(2):
            total = mine(0, side, h)
            for f in (first, second):
                if (f, h) in zlast:
                    zlast[f, h][0].wait_recv()
                    total = total + rbuf[zlast[f, h][1]].astype(F32)
            out[h * edge : (h + 1) * edge] = total

    def inner_terms(distances):
        for d in distances:
            gbuf[...] += grad_term(mine_both(d, side_a), g_of(d, 1))
            gbuf[...] += grad_term(mine_both(d, side_b), g_of(d, 0))

    gbuf[...] = jnp.zeros_like(gbuf)
    inner = sorted(range(1 - reach, reach), key=abs, reverse=True)
    emit_some(3)
    for distance in range(half, reach, -1):
        ring_step(distance)
        emit_some(len(pending) if distance <= reach + 2 else 4)
        if distance == reach + 2:
            inner_terms(inner[: reach - 1])
            inner = inner[reach - 1 :]
    emit_some(len(pending))
    if reach >= 1:
        inner_terms(inner)
        ring_step(reach, True)
    else:
        ring_end(side_a, 0, 1, xsend)
        over_x_pair = send(xsend, xrecv, x_s, x_r, x_peer)
        ring_end(side_b, 2, 3, mbuf)
        gbuf[...] = grad_term(xsend[...], g_of(0, 1)) + grad_term(mbuf[...], g_of(0, 0))

    used = [0]

    def farthest_first(m):
        return sorted(range(1, m), key=lambda d: -min(d, m - d))

    def pair():
        k = used[0]
        used[0] += 1
        return a_s.at[k], a_r.at[k]

    def total_of(slots_ref, m):
        total = slots_ref[0]
        for k in range(1, m):
            total = total + slots_ref[k]
        return total

    hrows = gbuf.shape[0] // 2
    here = pl.ds(pl.multiple_of(c * hrows, hrows), hrows)
    there = pl.ds(pl.multiple_of((1 - c) * hrows, hrows), hrows)
    first = send(gbuf.at[there], r1, *pair(), core_peer)
    first.wait_recv()
    hbuf[...] = (gbuf[here] + r1[...]).reshape(hbuf.shape)
    r2[y] = hbuf[y]
    over_y = [send(hbuf.at[lax.rem(y + d, ny)], r2.at[y], *pair(), y_peer(d)) for d in farthest_first(ny)]
    for distance in range(reach - 1, 0, -1):
        ring_step(distance)
    for copy in over_y:
        copy.wait_recv()
    vbuf[...] = total_of(r2, ny)
    r3[x] = vbuf[...]
    over_x = [send(vbuf, r3.at[x], *pair(), x4_peer(d)) for d in farthest_first(4)]
    if reach >= 1:
        ring_end(side_a, 0, 1, xsend)
        over_x_pair = send(xsend, xrecv, x_s, x_r, x_peer)
        ring_end(side_b, 2, 3, mbuf)
    for copy in over_x:
        copy.wait_recv()
    ubuf[...] = total_of(r3, 4)
    r4[z] = ubuf[...]
    over_z = [send(ubuf, r4.at[z], *pair(), z_peer(d)) for d in farthest_first(nz)]
    over_x_pair.wait_recv()
    aggregate = mbuf[...] + xrecv[...]
    mixed_ref[...] = jnp.dot(
        aggregate.astype(BF16), w_ref[...], preferred_element_type=F32
    ).astype(BF16)
    for copy in over_z:
        copy.wait_recv()
    tbuf[...] = total_of(r4, nz)
    r5[y] = tbuf[...]
    back = {d: send(tbuf, r5.at[y], *pair(), y_peer(d)) for d in farthest_first(ny)}
    other = [send(tbuf, r6.at[y], *pair(), core_peer)]
    for d in reversed(farthest_first(ny)):
        back[d].wait_recv()
        at = lax.rem(y - d + ny, ny)
        other.append(send(r5.at[at], r6.at[at], *pair(), core_peer))
    for copy in other:
        copy.wait_recv()
    grad_ref[here] = r5[...].reshape(hrows, -1)
    grad_ref[there] = r6[...].reshape(hrows, -1)
    for copy in started:
        copy.wait_send()


def body(node_features, layer_weight, tile_values, tile_positions, section_tile_count, out_cotangent):
    sections, cap, edge, _ = tile_values.shape[1:]
    ny = sections // XH
    nz = lax.axis_size("rep") // (XL * CORES)
    reach = min(2, nz // 2 - 1)
    slots = sections * cap
    f, h = layer_weight.shape
    rows = out_cotangent.shape[0]
    copies = 4 * (nz - 1)
    gathers = PIECES * (1 + 2 * (ny - 1))
    g_copies = 1 + 4 * reach
    hrows = f // 2
    piece = hrows // ny
    small = 1 + 2 * (ny - 1) + 3 + (nz - 1) + ny
    width = max(128, nz * 8)
    dma, vmem, smem = pltpu.SemaphoreType.DMA, pltpu.VMEM, pltpu.SMEM
    whole = pl.BlockSpec(memory_space=pltpu.VMEM)
    return pl.pallas_call(
        functools.partial(kernel, ny, nz, reach),
        out_shape=(
            jax.ShapeDtypeStruct((rows, h), BF16),
            jax.ShapeDtypeStruct((f, h), F32),
        ),
        in_specs=[whole, whole, pl.BlockSpec(memory_space=pl.ANY), whole, whole, whole],
        out_specs=(whole, whole),
        scratch_shapes=[
            vmem((sections, cap, edge, edge), BF16),
            vmem((sections, PIECES, rows // PIECES, f), BF16),
            vmem((2, slots, edge, f), F32),
            vmem((slots, edge, f), F32),
            vmem((1, slots), I32),
            vmem((1, width), I32),
            smem((1, slots), I32),
            smem((1, width), I32),
            vmem((2 * reach + 1, XL, rows, h), BF16),
            vmem((nz, XL, 2, edge, f), BF16),
            vmem((nz, XL, 2, edge, f), BF16),
            vmem((copies, edge, f), BF16),
            vmem((copies, edge, f), BF16),
            vmem((rows, f), F32),
            vmem((rows, f), F32),
            vmem((rows, f), F32),
            vmem((f, h), F32),
            vmem((hrows, h), F32),
            vmem((ny, piece, h), F32),
            vmem((ny, piece, h), F32),
            vmem((piece, h), F32),
            vmem((4, piece, h), F32),
            vmem((piece, h), F32),
            vmem((nz, piece, h), F32),
            vmem((piece, h), F32),
            vmem((ny, piece, h), F32),
            vmem((ny, piece, h), F32),
            dma, dma((2,)), dma((gathers,)), dma((gathers,)), dma((g_copies,)), dma((g_copies,)),
            dma((nz,)), dma((nz,)), dma((copies,)), dma((copies,)), dma, dma, dma((small,)), dma((small,)),
        ],
        compiler_params=pltpu.CompilerParams(
            collective_id=0, has_side_effects=True, vmem_limit_bytes=56 << 20
        ),
        name="graph_layer",
    )(node_features, layer_weight, tile_values[0], tile_positions, section_tile_count, out_cotangent)


def solution(mesh):
    placed = (
        P(("row", "rep"), None),
        P(),
        P("row", "rep", None, None, None),
        P("row", "rep", None),
        P("row", "rep"),
        P(("row", "rep"), None),
    )
    return jax.shard_map(
        body, mesh=mesh, in_specs=placed, out_specs=(P(("row", "rep"), None), P()), check_vma=False
    )
```

```python
import functools

import jax
import jax.numpy as jnp
from jax import lax
from jax.experimental import pallas as pl
from jax.experimental.pallas import tpu as pltpu
from jax.sharding import PartitionSpec as P

MESH = pl.DeviceIdType.MESH
F32, BF16, I32 = jnp.float32, jnp.bfloat16, jnp.int32
XH, XL, CORES = 2, 2, 2
PIECES = 2


def iota(shape, dim):
    return lax.broadcasted_iota(I32, shape, dim)


def sort_slots(pos, cnt, tiles_all, width):
    cap, n = pos.shape
    slots = n * cap
    slot = iota((cap, n), 0)
    key = jnp.where(slot < cnt, lax.div(pos, 2), tiles_all)
    code = (key * slots + iota((cap, n), 1) * cap + slot) * 2 + lax.rem(pos, 2)
    spread = jnp.broadcast_to(code[None, :, :], (n, cap, n))
    picked = jnp.where(iota((n, cap, n), 0) == iota((n, cap, n), 2), spread, 0)
    column = jnp.sum(picked, axis=2, keepdims=True).reshape(slots, 1)
    grid = jnp.broadcast_to(column, (slots, slots))
    lane = iota((slots, slots), 1)
    line = jnp.sum(jnp.where(iota((slots, slots), 0) == lane, grid, 0), axis=0, keepdims=True)
    rank = jnp.sum(jnp.where(line < grid, 1, 0), axis=1, keepdims=True)
    ordered = jnp.sum(jnp.where(rank == lane, grid, 0), axis=0, keepdims=True)
    rows = lax.div(jnp.broadcast_to(column, (slots, width)), 2 * slots)
    ends = jnp.sum(jnp.where(rows <= iota((slots, width), 1), 1, 0), axis=0, keepdims=True)
    return ordered, ends


def kernel(
    ny, nz, reach, x_ref, w_ref, tile_ref, pos_ref, cnt_ref, g_ref, mixed_ref, grad_ref,
    tiles, xall, prod, runs, codes_v, ends_v, codes, ends, gall, oth, cbuf, sbuf, rbuf, mbuf,
    xsend, xrecv, gbuf, r1, hbuf, r2, vbuf, r3, ubuf, r4, tbuf, r5, r6,
    t_s, i_s, ag_s, ag_r, g_s, g_r, c_s, c_r, z_s, z_r, x_s, x_r, a_s, a_r,
):
    row, rep = lax.axis_index("row"), lax.axis_index("rep")
    xh, y = row // ny, lax.rem(row, ny)
    z, xl, c = rep // 4, lax.rem(rep // 2, 2), lax.rem(rep, 2)
    x = xh * 2 + xl
    half, yhalf = nz // 2, ny // 2
    n, cap, edge = tiles.shape[0], tiles.shape[1], tiles.shape[2]
    slots = n * cap

    partner = ((1 - xh) * ny + y, rep)
    core_peer = (row, rep + 1 - 2 * c)
    x_peer = (row, z * 4 + (1 - xl) * 2 + c)

    def z_peer(d):
        return (row, lax.rem(z + d + nz, nz) * 4 + xl * 2 + c)

    def y_peer(d):
        return (xh * ny + lax.rem(y + d + ny, ny), rep)

    def x4_peer(d):
        q = lax.rem(x + d, 4)
        return ((q // 2) * ny + y, z * 4 + lax.rem(q, 2) * 2 + c)

    started = []

    def send(src, dst, s_sem, r_sem, peer):
        copy = pltpu.make_async_remote_copy(src, dst, s_sem, r_sem, device_id=peer, device_id_type=MESH)
        copy.start()
        started.append(copy)
        return copy

    load_tiles = pltpu.make_async_copy(tile_ref, tiles, t_s)
    load_tiles.start()
    barrier = pltpu.get_barrier_semaphore()
    peers = [partner, core_peer, x_peer, z_peer(1), y_peer(1)]
    if nz > 2:
        peers.append(z_peer(-1))
    if ny > 2:
        peers.append(y_peer(-1))
    for peer in peers:
        pl.semaphore_signal(barrier, inc=1, device_id=peer, device_id_type=MESH)
    tiles_all = nz * 8
    codes_v[...], ends_v[...] = sort_slots(pos_ref[0], cnt_ref[...], tiles_all, ends_v.shape[1])
    to_scalar = [pltpu.make_async_copy(codes_v, codes, i_s.at[0]), pltpu.make_async_copy(ends_v, ends, i_s.at[1])]
    for copy in to_scalar:
        copy.start()
    pl.semaphore_wait(barrier, len(peers))

    part = edge * 2 // PIECES
    gather_count = [0]

    def gather_send(src, slot, p, peer):
        k = gather_count[0]
        gather_count[0] += 1
        return send(src, xall.at[slot, p], ag_s.at[k], ag_r.at[k], peer)

    def slot_of(side, shift):
        return side * ny + lax.rem(y + shift + ny, ny)

    def product(slot, ref=None):
        if ref is None:
            both = jnp.concatenate([xall[slot, p] for p in range(PIECES)], axis=1)
        else:
            both = jnp.concatenate([ref[:edge], ref[edge:]], axis=1)

        def some(q, carry):
            out = jnp.dot(
                tiles[slot, pl.ds(q * 4, 4)].reshape(4 * edge, edge), both, preferred_element_type=F32
            )
            at = slot * cap + q * 4
            prod[0, pl.ds(at, 4)] = out[:, :edge].reshape(4, edge, edge)
            prod[1, pl.ds(at, 4)] = out[:, edge:].reshape(4, edge, edge)
            return carry

        lax.fori_loop(0, cap // 4, some, 0)

    g_count = [0]
    near, seen = {}, set()
    sides = (xl, 1 - xl)

    def g_send(src, d, side, x_lo, peer):
        k = g_count[0]
        g_count[0] += 1
        near[d, side] = send(src, gall.at[reach + d, x_lo], g_s.at[k], g_r.at[k], peer)

    def g_wait(d, side):
        if (d, side) not in seen:
            seen.add((d, side))
            near[d, side].wait_recv()

    chains, over = {}, {}

    def steps_of(side, way, p):
        return yhalf if ((way == 1) == (p == 0)) == (side == 0) else yhalf - 1

    def forward(side, way, p, distance):
        slot = slot_of(xh if side == 0 else 1 - xh, -way * distance)
        src = xall.at[slot, p]
        if distance == 0 and side == 0:
            src = x_ref.at[pl.ds(p * part, part)]
        elif distance > 0:
            chains[side, way, p].wait_recv()
        if distance < steps_of(side, way, p):
            chains[side, way, p] = gather_send(src, slot, p, y_peer(way))

    def send_g(hop):
        for zway in (1, -1):
            for side in range(2):
                g_wait(-zway * hop, side)
                g_send(
                    gall.at[reach - zway * hop, sides[side]],
                    -zway * (hop + 1), side, sides[side], z_peer(zway),
                )

    for p in range(PIECES):
        for way in (1, -1):
            forward(0, way, p, 0)
        over[p] = gather_send(x_ref.at[pl.ds(p * part, part)], row, p, partner)
    g_send(g_ref, 0, 1, xl, x_peer)
    if reach >= 1:
        for zway in (1, -1):
            g_send(g_ref, -zway, 0, xl, z_peer(zway))
    for p in range(PIECES):
        over[p].wait_recv()
        for way in (1, -1):
            forward(1, way, p, 0)
    load_tiles.wait()
    product(row, x_ref)
    product((1 - xh) * ny + y)
    for distance in range(1, yhalf + 1):
        ways = (1, -1) if distance < yhalf else (1,)
        for side in range(2):
            for p in range(PIECES):
                for way in (1, -1):
                    if distance <= steps_of(side, way, p):
                        forward(side, way, p, distance)
        for side in range(2):
            for way in ways:
                product(slot_of(xh if side == 0 else 1 - xh, -way * distance))
        if distance == min(2, yhalf) and reach >= 1:
            g_wait(0, 1)
            for zway in (1, -1):
                g_send(gall.at[reach, 1 - xl], -zway, 1, 1 - xl, z_peer(zway))
    for hop in range(1, reach):
        send_g(hop)

    for copy in to_scalar:
        copy.wait()

    def accumulate(k, run):
        code = codes[0, k]
        before = codes[0, jnp.maximum(k - 1, 0)]
        same = lax.div(code, 2 * slots) == lax.div(before, 2 * slots)
        run = prod[lax.rem(code, 2), lax.rem(lax.div(code, 2), slots)] + jnp.where(same, run, 0.0)
        runs[k] = run
        return run

    lax.fori_loop(0, slots, accumulate, jnp.zeros((edge, edge), F32), unroll=2)

    def tile_sum(t):
        upto = ends[0, t]
        below = jnp.where(t > 0, ends[0, jnp.maximum(t - 1, 0)], 0)
        return jnp.where(upto > below, runs[jnp.maximum(upto - 1, 0)], 0.0)

    def at_z(d):
        return lax.rem(z + d + nz, nz)

    order = [half]
    for d in range(half - 1, 0, -1):
        order += [d, -d]
    order.append(0)
    from_core, ready = {}, set()

    def emit(d):
        at = at_z(d)
        for side in range(XL):
            first = ((at * XL + side) * CORES + 1 - c) * 2
            for h in range(2):
                oth[at, side, h] = tile_sum(first + h).astype(BF16)
        k = len(from_core)
        from_core[d] = send(oth.at[at], cbuf.at[at], c_s.at[k], c_r.at[k], core_peer)

    pending = list(order)

    def emit_some(m):
        for _ in range(m):
            if pending:
                emit(pending.pop(0))

    def mine(d, side, h):
        if d == -half:
            d = half
        if d not in ready:
            from_core[d].wait_recv()
            ready.add(d)
        at = at_z(d)
        return tile_sum(((at * XL + side) * CORES + c) * 2 + h) + cbuf[at, side, h].astype(F32)

    def mine_both(d, side):
        return jnp.concatenate([mine(d, side, 0), mine(d, side, 1)], axis=0)

    def grad_term(m, g):
        high = m.astype(BF16)
        low = (m - high.astype(F32)).astype(BF16)
        total = None
        for v in (high, low):
            term = lax.dot_general(v, g, (((0,), (0,)), ((), ())), preferred_element_type=F32)
            total = term if total is None else total + term
        return total

    def g_of(d, side):
        if (d, side) == (0, 0):
            return g_ref[...]
        g_wait(d, side)
        return gall[reach + d, sides[side]]

    side_a, side_b = 1 - xl, xl
    zflows = [(0, 1, half), (0, -1, half - 1), (1, 1, half - 1), (1, -1, half)]
    zlast = {}
    count = [0]

    def ring_step(distance, terms=False):
        for f, (side, way, steps) in enumerate(zflows):
            if distance > steps:
                continue
            for h in range(2):
                total = mine(way * distance, side_a if side == 0 else side_b, h)
                if (f, h) in zlast:
                    zlast[f, h][0].wait_recv()
                    total = total + rbuf[zlast[f, h][1]].astype(F32)
                k = count[0]
                count[0] += 1
                sbuf[k] = total.astype(BF16)
                zlast[f, h] = (send(sbuf.at[k], rbuf.at[k], z_s.at[k], z_r.at[k], z_peer(way)), k)
                if terms:
                    mbuf[h * edge : (h + 1) * edge] = total
            if terms:
                gbuf[...] += grad_term(mbuf[...], g_of(way * reach, 1 if side == 0 else 0))

    def ring_end(side, first, second, out):
        for h in range(2):
            total = mine(0, side, h)
            for f in (first, second):
                if (f, h) in zlast:
                    zlast[f, h][0].wait_recv()
                    total = total + rbuf[zlast[f, h][1]].astype(F32)
            out[h * edge : (h + 1) * edge] = total

    def inner_terms(distances):
        for d in distances:
            gbuf[...] += grad_term(mine_both(d, side_a), g_of(d, 1))
            gbuf[...] += grad_term(mine_both(d, side_b), g_of(d, 0))

    gbuf[...] = jnp.zeros_like(gbuf)
    inner = sorted(range(1 - reach, reach), key=abs, reverse=True)
    emit_some(3)
    for distance in range(half, reach, -1):
        ring_step(distance)
        emit_some(len(pending) if distance <= reach + 2 else 4)
        if distance == reach + 2:
            inner_terms(inner[: reach - 1])
            inner = inner[reach - 1 :]
    emit_some(len(pending))
    if reach >= 1:
        inner_terms(inner)
        ring_step(reach, True)
    else:
        ring_end(side_a, 0, 1, xsend)
        over_x_pair = send(xsend, xrecv, x_s, x_r, x_peer)
        ring_end(side_b, 2, 3, mbuf)
        gbuf[...] = grad_term(xsend[...], g_of(0, 1)) + grad_term(mbuf[...], g_of(0, 0))

    used = [0]

    def farthest_first(m):
        return sorted(range(1, m), key=lambda d: -min(d, m - d))

    def pair():
        k = used[0]
        used[0] += 1
        return a_s.at[k], a_r.at[k]

    def total_of(slots_ref, m):
        total = slots_ref[0]
        for k in range(1, m):
            total = total + slots_ref[k]
        return total

    hrows = gbuf.shape[0] // 2
    here = pl.ds(pl.multiple_of(c * hrows, hrows), hrows)
    there = pl.ds(pl.multiple_of((1 - c) * hrows, hrows), hrows)
    first = send(gbuf.at[there], r1, *pair(), core_peer)
    first.wait_recv()
    hbuf[...] = (gbuf[here] + r1[...]).reshape(hbuf.shape)
    r2[y] = hbuf[y]
    over_y = [send(hbuf.at[lax.rem(y + d, ny)], r2.at[y], *pair(), y_peer(d)) for d in farthest_first(ny)]
    for distance in range(reach - 1, 0, -1):
        ring_step(distance)
    for copy in over_y:
        copy.wait_recv()
    vbuf[...] = total_of(r2, ny)
    r3[x] = vbuf[...]
    over_x = [send(vbuf, r3.at[x], *pair(), x4_peer(d)) for d in farthest_first(4)]
    if reach >= 1:
        ring_end(side_a, 0, 1, xsend)
        over_x_pair = send(xsend, xrecv, x_s, x_r, x_peer)
        ring_end(side_b, 2, 3, mbuf)
    for copy in over_x:
        copy.wait_recv()
    ubuf[...] = total_of(r3, 4)
    r4[z] = ubuf[...]
    over_z = [send(ubuf, r4.at[z], *pair(), z_peer(d)) for d in farthest_first(nz)]
    over_x_pair.wait_recv()
    aggregate = mbuf[...] + xrecv[...]
    mixed_ref[...] = jnp.dot(
        aggregate.astype(BF16), w_ref[...], preferred_element_type=F32
    ).astype(BF16)
    for copy in over_z:
        copy.wait_recv()
    tbuf[...] = total_of(r4, nz)
    r5[y] = tbuf[...]
    back = {d: send(tbuf, r5.at[y], *pair(), y_peer(d)) for d in farthest_first(ny)}
    other = [send(tbuf, r6.at[y], *pair(), core_peer)]
    for d in reversed(farthest_first(ny)):
        back[d].wait_recv()
        at = lax.rem(y - d + ny, ny)
        other.append(send(r5.at[at], r6.at[at], *pair(), core_peer))
    for copy in other:
        copy.wait_recv()
    grad_ref[here] = r5[...].reshape(hrows, -1)
    grad_ref[there] = r6[...].reshape(hrows, -1)
    for copy in started:
        copy.wait_send()


def body(node_features, layer_weight, tile_values, tile_positions, section_tile_count, out_cotangent):
    sections, cap, edge, _ = tile_values.shape[1:]
    ny = sections // XH
    nz = lax.axis_size("rep") // (XL * CORES)
    reach = min(2, nz // 2 - 1)
    slots = sections * cap
    f, h = layer_weight.shape
    rows = out_cotangent.shape[0]
    copies = 4 * (nz - 1)
    gathers = PIECES * (1 + 2 * (ny - 1))
    g_copies = 1 + 4 * reach
    hrows = f // 2
    piece = hrows // ny
    small = 1 + 2 * (ny - 1) + 3 + (nz - 1) + ny
    width = max(128, nz * 8)
    dma, vmem, smem = pltpu.SemaphoreType.DMA, pltpu.VMEM, pltpu.SMEM
    whole = pl.BlockSpec(memory_space=pltpu.VMEM)
    positions = jnp.swapaxes(tile_positions, 1, 2)
    return pl.pallas_call(
        functools.partial(kernel, ny, nz, reach),
        out_shape=(
            jax.ShapeDtypeStruct((rows, h), BF16),
            jax.ShapeDtypeStruct((f, h), F32),
        ),
        in_specs=[whole, whole, pl.BlockSpec(memory_space=pl.ANY), whole, whole, whole],
        out_specs=(whole, whole),
        scratch_shapes=[
            vmem((sections, cap, edge, edge), BF16),
            vmem((sections, PIECES, rows // PIECES, f), BF16),
            vmem((2, slots, edge, f), F32),
            vmem((slots, edge, f), F32),
            vmem((1, slots), I32),
            vmem((1, width), I32),
            smem((1, slots), I32),
            smem((1, width), I32),
            vmem((2 * reach + 1, XL, rows, h), BF16),
            vmem((nz, XL, 2, edge, f), BF16),
            vmem((nz, XL, 2, edge, f), BF16),
            vmem((copies, edge, f), BF16),
            vmem((copies, edge, f), BF16),
            vmem((rows, f), F32),
            vmem((rows, f), F32),
            vmem((rows, f), F32),
            vmem((f, h), F32),
            vmem((hrows, h), F32),
            vmem((ny, piece, h), F32),
            vmem((ny, piece, h), F32),
            vmem((piece, h), F32),
            vmem((4, piece, h), F32),
            vmem((piece, h), F32),
            vmem((nz, piece, h), F32),
            vmem((piece, h), F32),
            vmem((ny, piece, h), F32),
            vmem((ny, piece, h), F32),
            dma, dma((2,)), dma((gathers,)), dma((gathers,)), dma((g_copies,)), dma((g_copies,)),
            dma((nz,)), dma((nz,)), dma((copies,)), dma((copies,)), dma, dma, dma((small,)), dma((small,)),
        ],
        compiler_params=pltpu.CompilerParams(
            collective_id=0, has_side_effects=True, vmem_limit_bytes=56 << 20
        ),
        name="graph_layer",
    )(node_features, layer_weight, tile_values[0], positions, section_tile_count, out_cotangent)


def solution(mesh):
    placed = (
        P(("row", "rep"), None),
        P(),
        P("row", "rep", None, None, None),
        P("row", "rep", None),
        P("row", "rep"),
        P(("row", "rep"), None),
    )
    return jax.shard_map(
        body, mesh=mesh, in_specs=placed, out_specs=(P(("row", "rep"), None), P()), check_vma=False
    )
```
